256 devices in a mesh: ri: 16 (over z, core), ao: 16 (over x, y).
Axes of the slice: x: 4, y: 4, z: 8, core: 2. Of those that a mesh axis runs over, the one named last changes fastest.
Arguments:
- three_center: bfloat16 [256, 2048, 2048], P('ri', 'ao'), as said below
- slab_tensor: bfloat16 [32, 2048, 2048], P('ri', 'ao'), as said below
- occ_green: bfloat16 [2048, 2048], P('ao'), as said below
- virt_green: bfloat16 [2048, 2048], P('ao'), as said below
- pattern: int32 [128, 128], replicated, may hold values from 0 to 1, as said below
- atom_sizes: int32 [128], replicated, may hold values from 6 to 16, as said below
Outputs:
- polar_slab: float32 [256, 32], P('ri')
The draws below stay inside these ranges and needn't reach their ends.
Inputs may be any that keep to these rules, and one draw needn't show every extreme that they name: three_center is symmetric in its last two dimensions. slab_tensor is symmetric in its last two dimensions. `occ_green`: symmetric matrix. `virt_green`: symmetric matrix. `pattern`: symmetric 0/1 matrix with ones on the diagonal. `atom_sizes`: some atom block has all 16 functions live.
All inputs are finite; a program needn't handle non-finite values.
Results may differ from the reference program's by a relative error of at most 0.0041.
Values may be sent and summed in bfloat16 or wider, within the bound.
A program may use at most 128 MiB of HBM per device.

```python
import jax
import jax.numpy as jnp
from jax import lax

ATOM_BS = 16
RI_DEV = 16
NAO = 2048
RI = 256
SLAB = 32
NATOMS = 128
N_RI = 16


def symmetric_normal(rng_key, order):
    normals = jax.random.normal(rng_key, (order, order), jnp.float32)
    return (normals + normals.T) * 0.70710678


def tensor_rows(rng_key, row_total):

    def one_row(row_number):
        return symmetric_normal(jax.random.fold_in(rng_key, row_number), NAO).astype(jnp.bfloat16)
    return lax.map(one_row, jnp.arange(row_total, dtype=jnp.int32))


def draw_three_center(rng_key, part_index):
    return tensor_rows(jax.random.fold_in(rng_key, 11), RI)


def draw_slab_tensor(rng_key, part_index):
    return tensor_rows(jax.random.fold_in(rng_key, 12), SLAB)


def draw_occ_green(rng_key, part_index):
    values = symmetric_normal(jax.random.fold_in(rng_key, 13), NAO) / jnp.sqrt(jnp.float32(NAO))
    return values.astype(jnp.bfloat16)


def draw_virt_green(rng_key, part_index):
    values = symmetric_normal(jax.random.fold_in(rng_key, 14), NAO) / jnp.sqrt(jnp.float32(NAO))
    return values.astype(jnp.bfloat16)


def draw_pattern(rng_key, part_index):
    coin_flips = jax.random.randint(jax.random.fold_in(rng_key, 15), (NATOMS, NATOMS), 0, 2, jnp.int32)
    upper_half = jnp.triu(coin_flips, 1)
    return upper_half + upper_half.T + jnp.eye(NATOMS, dtype=jnp.int32)


def draw_atom_sizes(rng_key, part_index):
    atom_counts = jax.random.randint(jax.random.fold_in(rng_key, 16), (NATOMS,), 6, ATOM_BS + 1, jnp.int32)
    forced_atom = jax.random.randint(jax.random.fold_in(rng_key, 17), (), 0, NATOMS, jnp.int32)
    return jnp.where(jnp.arange(NATOMS, dtype=jnp.int32) == forced_atom, ATOM_BS, atom_counts)


def setup_inputs(seed: int = 0) -> dict:
    splits = jax.random.split(jax.random.key(seed), 7)
    return {
        "three_center": draw_three_center(jax.random.fold_in(splits[6], 71), 0),
        "slab_tensor": draw_slab_tensor(jax.random.fold_in(splits[6], 71), 0),
        "occ_green": draw_occ_green(jax.random.fold_in(splits[6], 71), 0),
        "virt_green": draw_virt_green(jax.random.fold_in(splits[6], 71), 0),
        "pattern": draw_pattern(jax.random.fold_in(splits[6], 71), 0),
        "atom_sizes": draw_atom_sizes(jax.random.fold_in(splits[6], 71), 0),
    }


def live_functions(atom_sizes):
    atom_count = atom_sizes.shape[0]
    per_slot = jnp.broadcast_to(atom_sizes[:, None], (atom_count, ATOM_BS)).reshape(-1)
    slot_ids = jnp.broadcast_to(jnp.arange(ATOM_BS, dtype=jnp.int32)[None, :], (atom_count, ATOM_BS)).reshape(-1)
    return (slot_ids < per_slot).astype(jnp.float32)


def expand_pattern(pattern_rows):
    row_atoms = pattern_rows.shape[0]
    col_atoms = pattern_rows.shape[1]
    grown = jnp.broadcast_to(pattern_rows[:, None, :, None], (row_atoms, ATOM_BS, col_atoms, ATOM_BS))
    return grown.reshape(row_atoms * ATOM_BS, col_atoms * ATOM_BS).astype(jnp.float32)


def reference(three_center, slab_tensor, occ_green, virt_green, pattern, atom_sizes):
    live_mask = live_functions(atom_sizes)
    screen = (expand_pattern(pattern) * live_mask[:, None] * live_mask[None, :]).astype(jnp.bfloat16)

    def slab_weight(one_slab):
        masked_slab = one_slab * screen
        left_product = jnp.dot(occ_green, masked_slab, preferred_element_type=jnp.float32).astype(jnp.bfloat16)
        return jnp.dot(left_product, virt_green.T, preferred_element_type=jnp.float32).astype(jnp.bfloat16)

    weighted = lax.map(slab_weight, slab_tensor)
    weight_flat = weighted.reshape(SLAB, NAO * NAO)
    blocks = three_center.reshape(N_RI, RI_DEV, NAO, NAO)

    def block_polar(block_in):
        masked_block = (block_in * screen[None]).reshape(RI_DEV, NAO * NAO)
        return jnp.dot(masked_block, weight_flat.T, preferred_element_type=jnp.float32)

    polar = lax.map(block_polar, blocks).reshape(RI, SLAB)
    return polar / NAO
```

```python
import functools

import jax
import jax.numpy as jnp
from jax import lax
from jax.experimental import pallas as pl
from jax.experimental.pallas import tpu as pltpu
from jax.sharding import PartitionSpec as P

MESH = pl.DeviceIdType.MESH
ATOM_BS = 16
NX, NY, NZ = 4, 4, 8
ROWS = 16

MIRRORED = ((1, 0), (1, 1), (1, 2), (1, 3), (0, 1), (2, 1))
PLAIN = ((0, 0), (0, 2), (2, 0), (2, 2))
OWNED = MIRRORED + PLAIN
NT = (((1,), (1,)), ((), ()))


def kernel(
    m_ref, s_ref, o_ref, v_ref, pat_ref, size_ref, out_ref,
    oh, vn, sg, lb, wb, fx1, fx2, tb, wz, mb, scr, part, red_s, red_x, red_y,
    ssem, rsem, lsem,
):
    blk, ao_total = o_ref.shape
    ri_rows = m_ref.shape[0]
    ri, ao = lax.axis_index("ri"), lax.axis_index("ao")
    z, core = ri // 2, ri % 2
    x, y = ao // NY, ao % NY

    def at_x(d):
        return (x + d) % NX

    def at_y(d):
        return (y + d) % NY

    def at_z(d):
        return (z + d) % NZ

    def dev(dx=0, dy=0, dz=0):
        return (at_z(dz) * 2 + core, at_x(dx) * NY + at_y(dy))

    sibling = (z * 2 + 1 - core, ao)
    half = blk // 2
    mine = pl.ds(pl.multiple_of(core * half, half), half)

    sent = []

    def send(src, dst, device):
        slot = len(sent)
        copy = pltpu.make_async_remote_copy(
            src_ref=src, dst_ref=dst, send_sem=ssem.at[slot], recv_sem=rsem.at[slot],
            device_id=device, device_id_type=MESH,
        )
        copy.start()
        sent.append(copy)
        return slot

    def arrived(ref, slot):
        pltpu.make_async_remote_copy(
            src_ref=ref, dst_ref=ref, send_sem=ssem.at[slot], recv_sem=rsem.at[slot],
            device_id=sibling, device_id_type=MESH,
        ).wait_recv()

    barrier = pltpu.get_barrier_semaphore()
    partners = [dev(dx=1), dev(dx=2), dev(dx=3), dev(dy=1), dev(dy=2), dev(dy=3), dev(dz=1), dev(dz=7), sibling]
    for partner in partners:
        pl.semaphore_signal(barrier, inc=1, device_id=partner, device_id_type=MESH)
    pl.semaphore_wait(barrier, len(partners))

    class Ring:
        def __init__(self, view, at, device, rows, start=0):
            self.view, self.at, self.device = view, at, device
            self.low = pl.ds(start, rows // 2)
            self.high = pl.ds(start + rows // 2, rows // 2)
            self.all = pl.ds(start, rows)

        def start(self, src=None):
            block = self.view(self.at(0), self.all)
            src = block if src is None else src
            self.a = send(src, block, self.device(1))
            self.b = send(src, block, self.device(3))

        def forward(self):
            arrived(self.view(self.at(3), self.all), self.a)
            piece = self.view(self.at(3), self.low)
            self.c = send(piece, piece, self.device(1))
            arrived(self.view(self.at(1), self.all), self.b)
            piece = self.view(self.at(1), self.high)
            self.d = send(piece, piece, self.device(3))

        def finish(self):
            arrived(self.view(self.at(2), self.low), self.c)
            arrived(self.view(self.at(2), self.high), self.d)

    def along_x(d):
        return dev(dx=d)

    def along_y(d):
        return dev(dy=d)

    class Shared(Ring):
        def share(self, d):
            piece = self.view(self.at(d), self.all)
            return send(piece, piece, sibling)

        def forward(self):
            super().forward()
            self.shared = [self.share(3), self.share(1)]

        def finish(self):
            super().finish()
            self.shared.append(self.share(2))

        def join(self):
            other = pl.ds(pl.multiple_of((1 - core) * half, half), half)
            for d, slot in zip((3, 1, 2), self.shared):
                arrived(self.view(self.at(d), other), slot)

    base = pl.multiple_of(core * half, half)
    o_ring = Shared(lambda i, r: oh.at[i, r], at_x, along_x, half, base)
    v_ring = Shared(lambda i, r: vn.at[i, r], at_y, along_y, half, base)
    s_rings = [Ring(lambda i, r, q=q: sg.at[q, i, r], at_y, along_y, blk) for q in range(2)]
    l_rings = [Ring(lambda i, r, q=q: lb.at[q, i, r], at_x, along_x, NX * blk) for q in range(2)]

    o_ring.start(o_ref.at[mine])

    atoms = pat_ref.shape[0]
    sizes = size_ref[...]
    row = lax.broadcasted_iota(jnp.int32, (blk, atoms), 0) + ao * blk
    row = row - lax.broadcasted_iota(jnp.int32, (blk, atoms), 1) * ATOM_BS
    grow_rows = jnp.where((row >= 0) & (row < sizes), 1.0, 0.0).astype(jnp.bfloat16)
    col = lax.broadcasted_iota(jnp.int32, (ao_total, atoms), 0)
    col = col - lax.broadcasted_iota(jnp.int32, (ao_total, atoms), 1) * ATOM_BS
    grow_cols = jnp.where((col >= 0) & (col < sizes), 1.0, 0.0).astype(jnp.bfloat16)
    pat = pat_ref[...].astype(jnp.float32).astype(jnp.bfloat16)
    pat_rows = jnp.dot(grow_rows, pat, preferred_element_type=jnp.float32).astype(jnp.bfloat16)
    screen = lax.dot_general(pat_rows, grow_cols, NT, preferred_element_type=jnp.float32)
    for b in range(NX * NY):
        scr[b] = screen[:, b * blk:(b + 1) * blk]
    for q in range(2):
        for b in range(NX * NY):
            cols = slice(b * blk, (b + 1) * blk)
            sg[q, y, :, cols] = (s_ref[q, :, cols].astype(jnp.float32) * scr[b]).astype(jnp.bfloat16)
        if q == 0:
            s_rings[0].start()

    locals_, m_slots = [], []
    for k, (dx, dy) in enumerate(OWNED):
        b = at_x(dx) * NY + at_y(dy)
        src = m_ref.at[:, :, pl.ds(pl.multiple_of(b * blk, blk), blk)]
        copy = pltpu.make_async_copy(src, mb.at[pl.ds(0, ri_rows), :, pl.ds(k * blk, blk)], lsem.at[k])
        copy.start()
        locals_.append(copy)
        m_slots.append(send(src, mb.at[pl.ds(ri_rows, ri_rows), :, pl.ds(k * blk, blk)], sibling))

    oh[x] = o_ref[...]
    vn[y] = v_ref[...]

    def left(q):
        product = lax.dot_general(
            oh[...].reshape(NX * blk, ao_total), sg[q].reshape(NY * blk, ao_total), NT,
            preferred_element_type=jnp.float32,
        )
        lb[q, x] = product.astype(jnp.bfloat16)

    def weighted(q):
        rows = jnp.concatenate([lb[q, i] for i in range(NX)], axis=1)
        product = lax.dot_general(
            rows, vn[...].reshape(NY * blk, ao_total), NT, preferred_element_type=jnp.float32
        ).astype(jnp.bfloat16)
        for i in range(NX):
            for j in range(NY):
                wb[q, i, j] = product[i * blk:(i + 1) * blk, j * blk:(j + 1) * blk]

    a_slots = {}

    def exchange(q):
        slots = {"x1": send(wb.at[q, at_x(3)], fx1.at[q], dev(dx=3))}
        for k, dy in enumerate((0, 1, 2)):
            slots["x2", k] = send(wb.at[q, at_x(2), at_y(dy)], fx2.at[q, k], dev(dx=2))
        for k, (dx, dy) in enumerate(MIRRORED):
            if dy:
                slots["t", k] = send(wb.at[q, at_x(dx), at_y(-dy % NY)], tb.at[q, k], dev(dy=-dy % NY))
        a_slots[q] = slots

    def assemble(q):
        slots = a_slots[q]
        arrived(fx1.at[q], slots["x1"])
        for k in range(3):
            arrived(fx2.at[q, k], slots["x2", k])
        for k, (dx, dy) in enumerate(MIRRORED):
            if dy:
                arrived(tb.at[q, k], slots["t", k])
        for k, (dx, dy) in enumerate(OWNED):
            if dx == 0:
                block = wb[q, x, at_y(dy)]
            elif dx == 1:
                block = fx1[q, at_y(dy)]
            else:
                block = fx2[q, dy]
            block = block.astype(jnp.float32)
            if k < len(MIRRORED):
                mirror = tb[q, k] if dy else wb[q, at_x(dx), y]
                block = block + mirror.astype(jnp.float32).T
            block = block * scr[at_x(dx) * NY + at_y(dy)]
            wz[z, q, :, k * blk:(k + 1) * blk] = block.astype(jnp.bfloat16)

    calls = []

    def contract(q, offsets):
        number = len(calls)
        width = ROWS * len(offsets)

        def step(i, total):
            rows = pl.ds(pl.multiple_of(i * ROWS, ROWS), ROWS)
            a = mb[:, rows, :].reshape(2 * ri_rows * ROWS, mb.shape[2])
            b = jnp.concatenate([wz[at_z(d), q, rows, :] for d in offsets], axis=0)
            return total + lax.dot_general(a, b, NT, preferred_element_type=jnp.float32)

        total = lax.fori_loop(0, blk // ROWS, step, jnp.zeros((2 * ri_rows * ROWS, width), jnp.float32))
        i = lax.broadcasted_iota(jnp.int32, total.shape, 0) % ROWS
        j = lax.broadcasted_iota(jnp.int32, total.shape, 1)
        total = jnp.where(i == j % ROWS, total, 0.0)
        total = jnp.sum(total.reshape(2 * ri_rows, ROWS, width), axis=1)
        unit = lax.broadcasted_iota(jnp.int32, (width, 128), 0) // ROWS
        column = lax.broadcasted_iota(jnp.int32, (width, 128), 1)
        place = jnp.zeros((width, 128), jnp.float32)
        for u, d in enumerate(offsets):
            place = jnp.where((unit == u) & (column == 4 * at_z(d) + 2 * core + q), 1.0, place)
        term = jnp.dot(total, place, precision=lax.Precision.HIGHEST, preferred_element_type=jnp.float32)
        part[...] = term if number == 0 else part[...] + term
        calls.append(number)

    z_slots = [{}, {}]

    def z_send(q, k):
        up, down = wz.at[at_z(1 - k), q], wz.at[at_z(k - 1), q]
        if k == NZ // 2:
            up = wz.at[at_z(1 - k), q, pl.ds(0, half)]
            down = wz.at[at_z(k - 1), q, pl.ds(half, half)]
        z_slots[q][k] = send(up, up, dev(dz=1)), send(down, down, dev(dz=7))

    def z_arrived(q, k):
        low, high = z_slots[q][k]
        if k == NZ // 2:
            arrived(wz.at[at_z(k), q, pl.ds(0, half)], low)
            arrived(wz.at[at_z(k), q, pl.ds(half, half)], high)
        else:
            arrived(wz.at[at_z(-k), q], low)
            arrived(wz.at[at_z(k), q], high)

    o_ring.forward()
    s_rings[0].forward()
    v_ring.start(v_ref.at[mine])
    s_rings[1].start()
    o_ring.finish()
    s_rings[0].finish()
    o_ring.join()
    left(0)
    l_rings[0].start()
    v_ring.forward()
    s_rings[1].forward()
    l_rings[0].forward()
    v_ring.finish()
    s_rings[1].finish()
    left(1)
    l_rings[1].start()
    v_ring.join()
    l_rings[0].finish()
    weighted(0)
    exchange(0)
    l_rings[1].forward()
    assemble(0)
    z_send(0, 1)
    for copy in locals_:
        copy.wait()
    for k, slot in enumerate(m_slots):
        arrived(mb.at[pl.ds(ri_rows, ri_rows), :, pl.ds(k * blk, blk)], slot)
    contract(0, (0,))
    l_rings[1].finish()
    weighted(1)
    exchange(1)
    z_arrived(0, 1)
    z_send(0, 2)
    assemble(1)
    z_send(1, 1)
    contract(1, (0,))
    contract(0, (7, 1))
    for k in range(2, NZ // 2 + 1):
        z_arrived(0, k)
        if k < NZ // 2:
            z_send(0, k + 1)
        z_arrived(1, k - 1)
        z_send(1, k)
        contract(0, (NZ - k, k) if k < NZ // 2 else (k,))
        contract(1, (NZ - k + 1, k - 1))
    z_arrived(1, NZ // 2)
    contract(1, (NZ // 2,))

    slot = send(part.at[pl.ds(ri_rows, ri_rows)], red_s, sibling)
    arrived(red_s, slot)
    red_x[x] = part[:ri_rows] + red_s[...]
    slots = [send(red_x.at[x], red_x.at[x], dev(dx=d)) for d in (1, 2, 3)]
    for d, slot in zip((1, 2, 3), slots):
        arrived(red_x.at[at_x(-d % NX)], slot)
    red_y[y] = red_x[0] + red_x[1] + red_x[2] + red_x[3]
    slots = [send(red_y.at[y], red_y.at[y], dev(dy=d)) for d in (1, 2, 3)]
    for d, slot in zip((1, 2, 3), slots):
        arrived(red_y.at[at_y(-d % NY)], slot)
    total = red_y[0] + red_y[1] + red_y[2] + red_y[3]
    out_ref[...] = total[:, :out_ref.shape[1]] / ao_total
    for copy in sent:
        copy.wait_send()


def shards(three_center, slab_tensor, occ_green, virt_green, pattern, atom_sizes):
    ri_rows, blk, ao_total = three_center.shape
    n_owned, n_mirrored = len(OWNED), len(MIRRORED)
    bf16, f32 = jnp.bfloat16, jnp.float32
    vmem = pl.BlockSpec(memory_space=pltpu.VMEM)
    columns = 4 * NZ
    return pl.pallas_call(
        kernel,
        out_shape=jax.ShapeDtypeStruct((ri_rows, columns), f32),
        in_specs=[pl.BlockSpec(memory_space=pl.ANY)] + [vmem] * 5,
        out_specs=vmem,
        scratch_shapes=[
            pltpu.VMEM((NX, blk, ao_total), bf16),
            pltpu.VMEM((NY, blk, ao_total), bf16),
            pltpu.VMEM((2, NY, blk, ao_total), bf16),
            pltpu.VMEM((2, NX, NX * blk, NY * blk), bf16),
            pltpu.VMEM((2, NX, NY, blk, blk), bf16),
            pltpu.VMEM((2, NY, blk, blk), bf16),
            pltpu.VMEM((2, 3, blk, blk), bf16),
            pltpu.VMEM((2, n_mirrored, blk, blk), bf16),
            pltpu.VMEM((NZ, 2, blk, n_owned * blk), bf16),
            pltpu.VMEM((2 * ri_rows, blk, n_owned * blk), bf16),
            pltpu.VMEM((NX * NY, blk, blk), f32),
            pltpu.VMEM((2 * ri_rows, 128), f32),
            pltpu.VMEM((ri_rows, 128), f32),
            pltpu.VMEM((NX, ri_rows, 128), f32),
            pltpu.VMEM((NY, ri_rows, 128), f32),
            pltpu.SemaphoreType.DMA((96,)),
            pltpu.SemaphoreType.DMA((96,)),
            pltpu.SemaphoreType.DMA((n_owned,)),
        ],
        compiler_params=pltpu.CompilerParams(
            collective_id=0, has_side_effects=True, vmem_limit_bytes=60 * 1024 * 1024
        ),
        name="polar_slab",
    )(three_center, slab_tensor, occ_green, virt_green, pattern, atom_sizes.reshape(1, -1))


def solution(mesh):
    placed = (P("ri", "ao", None), P("ri", "ao", None), P("ao", None), P("ao", None), P(), P())
    return jax.shard_map(
        shards, mesh=mesh, in_specs=placed, out_specs=P("ri", None), check_vma=False
    )
```

```python
import functools

import jax
import jax.numpy as jnp
from jax import lax
from jax.experimental import pallas as pl
from jax.experimental.pallas import tpu as pltpu
from jax.sharding import PartitionSpec as P

MESH = pl.DeviceIdType.MESH
ATOM_BS = 16
NX, NY, NZ = 4, 4, 8
ROWS = 16
CHUNKS = 4
SEMS = 96
V_PARTS = 4

MIRRORED = ((1, 0), (3, 3), (1, 3), (3, 2), (0, 1), (2, 1))
N_MAIN = len(MIRRORED) + 2
N_OWNED = N_MAIN + 1
TRAVEL = 6
NT = (((1,), (1,)), ((), ()))


def kernel(
    m_ref, s_ref, o_ref, v_ref, pat_ref, size_ref, out_ref,
    oh, vn, sg, lb, wb, ab0, ab1, wz0, wz1, mb, scr, gram, part, red_x, red_y,
    ssem, rsem, lsem,
):
    blk, ao_total = o_ref.shape
    ri_rows = m_ref.shape[0]
    ri, ao = lax.axis_index("ri"), lax.axis_index("ao")
    z, core = ri // 2, ri % 2
    x, y = ao // NY, ao % NY

    def at_x(d):
        return (x + d) % NX

    def at_y(d):
        return (y + d) % NY

    def at_z(d):
        return (z + d) % NZ

    def dev(dx=0, dy=0, dz=0):
        return (at_z(dz) * 2 + core, at_x(dx) * NY + at_y(dy))

    def other_core(dx):
        return (z * 2 + 1 - core, at_x(dx) * NY + y)

    sibling = (z * 2 + 1 - core, ao)
    half = blk // 2
    mine = pl.ds(pl.multiple_of(core * half, half), half)

    sent = []

    def remote(src, dst, device, slot):
        return pltpu.make_async_remote_copy(
            src_ref=src, dst_ref=dst, send_sem=ssem.at[slot], recv_sem=rsem.at[slot],
            device_id=device, device_id_type=MESH,
        )

    def group(whole):
        sent.append(remote(whole, whole, sibling, len(sent)))
        return len(sent) - 1

    def send(src, dst, device, slot=None):
        if slot is None:
            slot = len(sent)
            sent.append(remote(src, dst, device, slot))
        remote(src, dst, device, slot).start()
        return slot

    flushed = [0]

    def flush(keep=0):
        for copy in sent[flushed[0]:len(sent) - keep]:
            copy.wait_send()
        flushed[0] = len(sent) - keep

    def arrived(ref, slot):
        remote(ref, ref, sibling, slot).wait_recv()

    barrier = pltpu.get_barrier_semaphore()
    partners = [dev(dx=1), dev(dx=2), dev(dx=3), dev(dy=1), dev(dy=2), dev(dy=3), sibling]
    partners += [dev(dz=1), dev(dz=7)]
    partners += [other_core(1), other_core(2), other_core(3)]
    for partner in partners:
        pl.semaphore_signal(barrier, inc=1, device_id=partner, device_id_type=MESH)

    class Ring:
        def __init__(self, view, at, device, rows, start=0):
            self.view, self.at, self.device = view, at, device
            self.low = pl.ds(start, rows // 2)
            self.high = pl.ds(start + rows // 2, rows // 2)
            self.all = pl.ds(start, rows)

        def start(self, src=None):
            block = self.view(self.at(0), self.all)
            src = block if src is None else src
            self.a = send(src, block, self.device(1))
            self.b = send(src, block, self.device(3))

        def forward(self):
            arrived(self.view(self.at(3), self.all), self.a)
            piece = self.view(self.at(3), self.low)
            self.c = group(self.view(self.at(2), self.all))
            send(piece, piece, self.device(1), self.c)
            arrived(self.view(self.at(1), self.all), self.b)
            piece = self.view(self.at(1), self.high)
            send(piece, piece, self.device(3), self.c)

        def finish(self):
            arrived(self.view(self.at(2), self.all), self.c)

    def along_x(d):
        return dev(dx=d)

    def along_y(d):
        return dev(dy=d)

    base = pl.multiple_of(core * half, half)
    other = pl.ds(pl.multiple_of((1 - core) * half, half), half)
    v_width = ao_total // V_PARTS

    def v_part(i):
        return pl.ds(pl.multiple_of(i * v_width, v_width), v_width)

    v_cols = v_part(z % V_PARTS)
    c_rows = blk // CHUNKS
    n_chunks = 2 * CHUNKS

    o_ring = Ring(lambda i, r: oh.at[i, r], at_x, along_x, half, base)
    v_ring = Ring(lambda i, r: vn.at[i, r, v_cols], at_y, along_y, half, base)
    vz_ring = Ring(
        lambda i, r: vn.at[:, r, v_part(i)], lambda d: (z + d) % V_PARTS,
        lambda d: dev(dz=1 if d == 1 else NZ - 1), half, base,
    )
    s_rings, l_rings = [], []
    for t in range(n_chunks):
        q, start = t // CHUNKS, t % CHUNKS * c_rows
        s_rings.append(Ring(lambda i, r, q=q: sg.at[q, i, r], at_y, along_y, c_rows, start))
        l_rings.append(
            Ring(lambda i, r, q=q, start=start: lb.at[q, i, r, pl.ds(start, c_rows)], at_x, along_x, NY)
        )

    atoms = pat_ref.shape[0]
    sizes = size_ref[...]
    row = lax.broadcasted_iota(jnp.int32, (blk, atoms), 0) + ao * blk
    row = row - lax.broadcasted_iota(jnp.int32, (blk, atoms), 1) * ATOM_BS
    grow_rows = jnp.where((row >= 0) & (row < sizes), 1.0, 0.0).astype(jnp.bfloat16)
    col = lax.broadcasted_iota(jnp.int32, (ao_total, atoms), 0)
    col = col - lax.broadcasted_iota(jnp.int32, (ao_total, atoms), 1) * ATOM_BS
    grow_cols = jnp.where((col >= 0) & (col < sizes), 1.0, 0.0).astype(jnp.bfloat16)
    pat = pat_ref[...].astype(jnp.float32).astype(jnp.bfloat16)
    pat_rows = jnp.dot(grow_rows, pat, preferred_element_type=jnp.float32).astype(jnp.bfloat16)
    screen = lax.dot_general(pat_rows, grow_cols, NT, preferred_element_type=jnp.float32)
    for b in range(NX * NY):
        scr[b] = screen[:, b * blk:(b + 1) * blk]

    def mask(q):
        for b in range(NX * NY):
            cols = slice(b * blk, (b + 1) * blk)
            sg[q, y, :, cols] = (s_ref[q, :, cols].astype(jnp.float32) * scr[b]).astype(jnp.bfloat16)

    mask(0)
    oh[x] = o_ref[...]
    v_own = pltpu.make_async_copy(v_ref.at[mine, v_cols], vn.at[y, mine, v_cols], lsem.at[1])
    v_own.start()

    o_slots, v_slots, m_slots = [], [], []

    def o_share(d):
        piece = oh.at[at_x(d), mine]
        o_slots.append(send(piece, piece, sibling))

    def o_join():
        for d, slot in zip((3, 1, 2), o_slots):
            arrived(oh.at[at_x(d), other], slot)

    def v_share():
        piece = vn.at[:, mine]
        v_slots.append(send(piece, piece, sibling))

    def v_join():
        arrived(vn.at[:, other], v_slots[-1])

    far_x = at_x(2 * (y // 2))
    far_q = x // 2
    blocks = [at_x(dx) * NY + at_y(dy) for dx, dy in MIRRORED + ((0, 0),)]
    blocks += [far_x * NY + at_y(2), at_x(2) * NY + y]
    m_own, m_other = mb.at[pl.ds(0, ri_rows)], mb.at[pl.ds(ri_rows, ri_rows)]

    def m_start():
        m_slots.append(group(m_other))
        for k, b in enumerate(blocks):
            src = m_ref.at[:, :, pl.ds(pl.multiple_of(b * blk, blk), blk)]
            cols = pl.ds(k * blk, blk)
            pltpu.make_async_copy(src, mb.at[pl.ds(0, ri_rows), :, cols], lsem.at[0]).start()
            send(src, mb.at[pl.ds(ri_rows, ri_rows), :, cols], sibling, m_slots[0])

    def m_join():
        pltpu.make_async_copy(m_own, m_own, lsem.at[0]).wait()
        arrived(m_other, m_slots[0])

    def left(t):
        q, rows = t // CHUNKS, pl.ds(t % CHUNKS * c_rows, c_rows)
        product = lax.dot_general(
            sg[q, :, rows, :].reshape(NY * c_rows, ao_total), oh[...].reshape(NX * blk, ao_total), NT,
            preferred_element_type=jnp.float32,
        )
        lb[q, x, :, rows, :] = product.astype(jnp.bfloat16).reshape(NY, c_rows, NX * blk)

    def weighted(q):
        product = jnp.dot(
            vn[...].reshape(NY * blk, ao_total), lb[q].reshape(ao_total, NX * blk),
            preferred_element_type=jnp.float32,
        ).astype(jnp.bfloat16)
        for i in range(NX):
            for j in range(NY):
                wb[q, i, j] = product[j * blk:(j + 1) * blk, i * blk:(i + 1) * blk]

    a_slots = {}
    travel = (ab0, ab1)
    wz = (wz0, wz1)

    def exchange(q):
        slot = a_slots[q] = group(travel[q])
        along_x_, along_y_ = 0, TRAVEL
        for dx, dy in MIRRORED:
            if dx:
                send(wb.at[q, at_x(NX - dx), at_y(dy)], travel[q].at[along_x_], dev(dx=NX - dx), slot)
                along_x_ += 1
            if dy:
                send(wb.at[q, at_x(dx), at_y(NY - dy)], travel[q].at[along_y_], dev(dy=NY - dy), slot)
                along_y_ += 1
        send(wb.at[q, at_x(2), at_y(2)], travel[q].at[along_x_], dev(dx=2), slot)
        send(wb.at[q, at_x(2 - 2 * (y // 2)), at_y(2)], travel[q].at[along_y_], dev(dy=2), slot)
        if q == 1:
            send(wb.at[1 - far_q, at_x(2), y], travel[q].at[2 * TRAVEL], dev(dx=2), slot)

    def assemble(q):
        arrived(travel[q], a_slots[q])

        def put(k, block):
            cols = slice(k * blk, (k + 1) * blk)
            wz[q][z, :, cols] = (block * scr[blocks[k]]).astype(jnp.bfloat16)

        def wide(block):
            return block.astype(jnp.float32)

        along_x_, along_y_ = 0, TRAVEL
        for k, (dx, dy) in enumerate(MIRRORED):
            direct = travel[q][along_x_] if dx else wb[q, x, at_y(dy)]
            turned = travel[q][along_y_] if dy else wb[q, at_x(dx), y]
            along_x_, along_y_ = along_x_ + (dx > 0), along_y_ + (dy > 0)
            put(k, wide(direct).T + wide(turned))
        put(len(MIRRORED), wide(wb[q, x, y]).T)
        near = jnp.where(y < 2, 1.0, 0.0)
        direct = wide(wb[q, x, at_y(2)]) * near + wide(travel[q][along_x_]) * (1.0 - near)
        put(len(MIRRORED) + 1, direct.T + wide(travel[q][along_y_]))
        if q == 1:
            put(N_MAIN, wide(travel[q][2 * TRAVEL]).T + wide(wb[far_q, at_x(2), y]))

    gram[...] = jnp.zeros_like(gram)
    pairs = 2 * ri_rows * ROWS

    def contract(*units):
        units = sorted(units)
        second = [d for q, d in units if q == 1]
        main = N_MAIN * blk

        def step(i, totals):
            rows = pl.ds(pl.multiple_of(i * ROWS, ROWS), ROWS)
            b = jnp.concatenate([wz[q][at_z(d), rows, :main] for q, d in units], axis=0)
            a = mb[:, rows, :main].reshape(pairs, main)
            sums = [totals[0] + lax.dot_general(b, a, NT, preferred_element_type=jnp.float32)]
            if second:
                b = jnp.concatenate([wz1[at_z(d), rows, main:] for d in second], axis=0)
                a = mb[:, rows, main:].reshape(pairs, blk)
                sums.append(totals[1] + lax.dot_general(b, a, NT, preferred_element_type=jnp.float32))
            return sums

        heights = [ROWS * len(units)] + [ROWS * len(second)] * bool(second)
        totals = [jnp.zeros((height, pairs), jnp.float32) for height in heights]
        totals = lax.fori_loop(0, blk // ROWS, step, totals)
        places = [units, [(far_q, d) for d in second]]
        for total, where in zip(totals, places):
            i = lax.broadcasted_iota(jnp.int32, total.shape, 0) % ROWS
            j = lax.broadcasted_iota(jnp.int32, total.shape, 1) % ROWS
            total = jnp.where(i == j, total, 0.0)
            for u, (q, d) in enumerate(where):
                kept = jnp.sum(total[u * ROWS:(u + 1) * ROWS], axis=0, keepdims=True)
                row = pl.ds(4 * at_z(d) + 2 * core + q, 1)
                gram[row, :] = gram[row, :] + kept

    z_slots = [{}, {}]
    low, high = pl.ds(0, half), pl.ds(half, half)

    def z_send(q, k):
        up, down = wz[q].at[at_z(1 - k)], wz[q].at[at_z(k - 1)]
        if k < NZ // 2:
            z_slots[q][k] = send(up, up, dev(dz=1)), send(down, down, dev(dz=NZ - 1))
        else:
            slot = z_slots[q][k] = group(wz[q].at[at_z(k)])
            up, down = wz[q].at[at_z(1 - k), low], wz[q].at[at_z(k - 1), high]
            send(up, up, dev(dz=1), slot)
            send(down, down, dev(dz=NZ - 1), slot)

    def z_arrived(q, k):
        if k < NZ // 2:
            arrived(wz[q].at[at_z(-k)], z_slots[q][k][0])
            arrived(wz[q].at[at_z(k)], z_slots[q][k][1])
        else:
            arrived(wz[q].at[at_z(k)], z_slots[q][k])

    pl.semaphore_wait(barrier, len(partners))
    v_ring.start(v_ref.at[mine, v_cols])
    s_rings[0].start()
    o_ring.start(o_ref.at[mine])
    mask(1)
    for t in range(n_chunks + 3):
        if t < n_chunks:
            s_rings[t].forward()
        if t == 0:
            v_ring.forward()
            s_rings[1].start()
        if t + 2 < n_chunks:
            s_rings[t + 2].start()
        if t == 0:
            o_ring.forward()
            o_share(3)
            o_share(1)
            v_ring.finish()
            v_own.wait()
            vz_ring.start()
            o_ring.finish()
            o_share(2)
        if t == 1:
            o_join()
        if 1 <= t <= n_chunks:
            s_rings[t - 1].finish()
            left(t - 1)
            l_rings[t - 1].start()
        if t == 2:
            vz_ring.forward()
        if t == 3:
            vz_ring.finish()
            v_share()
        if 2 <= t <= n_chunks + 1:
            l_rings[t - 2].forward()
        if 3 <= t:
            l_rings[t - 3].finish()
        if t == 4:
            m_start()
        if t == CHUNKS + 2:
            v_join()
            weighted(0)
            exchange(0)
        if t == CHUNKS + 3:
            assemble(0)
            z_send(0, 1)
        if t == CHUNKS + 5:
            z_arrived(0, 1)
            z_send(0, 2)
    weighted(1)
    exchange(1)
    z_arrived(0, 2)
    z_send(0, 3)
    assemble(1)
    z_send(1, 1)
    m_join()
    contract((0, 0), (0, 7), (0, 1), (0, 6), (0, 2))
    z_arrived(0, 3)
    z_send(0, 4)
    z_arrived(1, 1)
    z_send(1, 2)
    contract((0, 5), (0, 3), (1, 0), (1, 7), (1, 1))
    flush(6)
    z_arrived(0, 4)
    z_arrived(1, 2)
    z_send(1, 3)
    contract((0, 4), (1, 6), (1, 2))
    z_arrived(1, 3)
    z_send(1, 4)
    contract((1, 5), (1, 3))
    flush(3)
    z_arrived(1, 4)
    contract((1, 4),)
    member = lax.broadcasted_iota(jnp.int32, (2 * ri_rows, pairs), 1) // ROWS
    member = member == lax.broadcasted_iota(jnp.int32, (2 * ri_rows, pairs), 0)
    part[...] = lax.dot_general(
        jnp.where(member, 1.0, 0.0), gram[...], NT, precision=lax.Precision.HIGHEST,
        preferred_element_type=jnp.float32,
    )

    own, theirs = part.at[pl.ds(0, ri_rows)], part.at[pl.ds(ri_rows, ri_rows)]
    red_x[core, x] = part[:ri_rows]
    place = red_x.at[core, x]
    slots = [send(own, place, dev(dx=d)) for d in (1, 2, 3)]
    slots += [send(theirs, place, other_core(d)) for d in range(NX)]
    for d, slot in zip((1, 2, 3), slots[:3]):
        arrived(red_x.at[core, at_x(NX - d)], slot)
    for d, slot in zip(range(NX), slots[3:]):
        arrived(red_x.at[1 - core, at_x(-d % NX)], slot)
    red_y[y] = functools.reduce(jnp.add, [red_x[i, j] for i in range(2) for j in range(NX)])
    slots = [send(red_y.at[y], red_y.at[y], dev(dy=d)) for d in (1, 2, 3)]
    for d, slot in zip((1, 2, 3), slots):
        arrived(red_y.at[at_y(NY - d)], slot)
    total = red_y[0] + red_y[1] + red_y[2] + red_y[3]
    out_ref[...] = total[:, :out_ref.shape[1]] / ao_total
    flush()


def shards(three_center, slab_tensor, occ_green, virt_green, pattern, atom_sizes):
    ri_rows, blk, ao_total = three_center.shape
    bf16, f32 = jnp.bfloat16, jnp.float32
    vmem = pl.BlockSpec(memory_space=pltpu.VMEM)
    columns = 4 * NZ
    return pl.pallas_call(
        kernel,
        out_shape=jax.ShapeDtypeStruct((ri_rows, columns), f32),
        in_specs=[pl.BlockSpec(memory_space=pl.ANY)] + [vmem] * 5,
        out_specs=vmem,
        scratch_shapes=[
            pltpu.VMEM((NX, blk, ao_total), bf16),
            pltpu.VMEM((NY, blk, ao_total), bf16),
            pltpu.VMEM((2, NY, blk, ao_total), bf16),
            pltpu.VMEM((2, NX, NY, blk, NX * blk), bf16),
            pltpu.VMEM((2, NX, NY, blk, blk), bf16),
            pltpu.VMEM((2 * TRAVEL, blk, blk), bf16),
            pltpu.VMEM((2 * TRAVEL + 1, blk, blk), bf16),
            pltpu.VMEM((NZ, blk, N_MAIN * blk), bf16),
            pltpu.VMEM((NZ, blk, N_OWNED * blk), bf16),
            pltpu.VMEM((2 * ri_rows, blk, N_OWNED * blk), bf16),
            pltpu.VMEM((NX * NY, blk, blk), f32),
            pltpu.VMEM((128, 2 * ri_rows * ROWS), f32),
            pltpu.VMEM((2 * ri_rows, 128), f32),
            pltpu.VMEM((2, NX, ri_rows, 128), f32),
            pltpu.VMEM((NY, ri_rows, 128), f32),
            pltpu.SemaphoreType.DMA((SEMS,)),
            pltpu.SemaphoreType.DMA((SEMS,)),
            pltpu.SemaphoreType.DMA((2,)),
        ],
        compiler_params=pltpu.CompilerParams(
            collective_id=0, has_side_effects=True, vmem_limit_bytes=60 * 1024 * 1024
        ),
        name="polar_slab",
    )(three_center, slab_tensor, occ_green, virt_green, pattern, atom_sizes.reshape(1, -1))


def solution(mesh):
    placed = (P("ri", "ao", None), P("ri", "ao", None), P("ao", None), P("ao", None), P(), P())
    return jax.shard_map(
        shards, mesh=mesh, in_specs=placed, out_specs=P("ri", None), check_vma=False
    )
```

```python
import functools

import jax
import jax.numpy as jnp
from jax import lax
from jax.experimental import pallas as pl
from jax.experimental.pallas import tpu as pltpu
from jax.sharding import PartitionSpec as P

MESH = pl.DeviceIdType.MESH
ATOM_BS = 16
NX, NY, NZ = 4, 4, 8
ROWS = 16
CHUNKS = 4
ARRIVALS, BOXES = 87, 14
V_PARTS = 4

MIRRORED = ((1, 0), (1, 1), (1, 3), (1, 2), (0, 1), (2, 1))
N_MAIN = len(MIRRORED) + 2
N_OWNED = N_MAIN + 1
TRAVEL = 6
NT = (((1,), (1,)), ((), ()))


def kernel(
    m_ref, s_ref, o_ref, v_ref, pat_ref, size_ref, out_ref,
    oh, vn, sg, lb, wb, ab0, ab1, wz0, wz1, mb, scr, gram, part, red_x, red_y,
    ssem, rsem, lsem,
):
    blk, ao_total = o_ref.shape
    ri_rows = m_ref.shape[0]
    ri, ao = lax.axis_index("ri"), lax.axis_index("ao")
    z, core = ri // 2, ri % 2
    x, y = ao // NY, ao % NY

    def at_x(d):
        return (x + d) % NX

    def at_y(d):
        return (y + d) % NY

    def at_z(d):
        return (z + d) % NZ

    def dev(dx=0, dy=0, dz=0):
        return (at_z(dz) * 2 + core, at_x(dx) * NY + at_y(dy))

    def other_core(dx):
        return (z * 2 + 1 - core, at_x(dx) * NY + y)

    sibling = (z * 2 + 1 - core, ao)
    half = blk // 2
    mine = pl.ds(pl.multiple_of(core * half, half), half)

    landed, boxes, emptied = [0], [], [0]

    def remote(src, dst, device, slot, box):
        return pltpu.make_async_remote_copy(
            src_ref=src, dst_ref=dst, send_sem=ssem.at[box], recv_sem=rsem.at[slot],
            device_id=device, device_id_type=MESH,
        )

    def outbox(whole):
        boxes.append(whole)
        return len(boxes) - 1

    def take():
        landed[0] += 1
        return landed[0] - 1

    def send(src, dst, device, box, slot=None):
        slot = take() if slot is None else slot
        remote(src, dst, device, slot, box).start()
        return slot

    def flush(last=None):
        for box in range(emptied[0], len(boxes) if last is None else last + 1):
            remote(boxes[box], boxes[box], sibling, 0, box).wait_send()
            emptied[0] = box + 1

    def arrived(ref, slot):
        remote(ref, ref, sibling, slot, 0).wait_recv()

    barrier = pltpu.get_barrier_semaphore()
    partners = [dev(dx=1), dev(dx=2), dev(dx=3), dev(dy=1), dev(dy=2), dev(dy=3), sibling]
    partners += [dev(dz=1), dev(dz=7)]
    partners += [other_core(1), other_core(2), other_core(3)]
    for partner in partners:
        pl.semaphore_signal(barrier, inc=1, device_id=partner, device_id_type=MESH)

    class Ring:
        def __init__(self, view, at, device, box, rows, start=0):
            self.view, self.at, self.device, self.box = view, at, device, box
            self.low = pl.ds(start, rows // 2)
            self.high = pl.ds(start + rows // 2, rows // 2)
            self.all = pl.ds(start, rows)

        def start(self, src=None):
            block = self.view(self.at(0), self.all)
            src = block if src is None else src
            self.a = send(src, block, self.device(1), self.box)
            self.b = send(src, block, self.device(3), self.box)

        def forward(self):
            arrived(self.view(self.at(3), self.all), self.a)
            piece = self.view(self.at(3), self.low)
            self.c = send(piece, piece, self.device(1), self.box)
            arrived(self.view(self.at(1), self.all), self.b)
            piece = self.view(self.at(1), self.high)
            send(piece, piece, self.device(3), self.box, self.c)

        def finish(self):
            arrived(self.view(self.at(2), self.all), self.c)

    def along_x(d):
        return dev(dx=d)

    def along_y(d):
        return dev(dy=d)

    base = pl.multiple_of(core * half, half)
    other = pl.ds(pl.multiple_of((1 - core) * half, half), half)
    v_width = ao_total // V_PARTS

    def v_part(i):
        return pl.ds(pl.multiple_of(i * v_width, v_width), v_width)

    v_cols = v_part(z % V_PARTS)
    c_rows = blk // CHUNKS
    n_chunks = 2 * CHUNKS

    quarter = half // 2
    o_box = outbox(oh.at[pl.ds(0, 3)])
    o_rings = [
        Ring(lambda i, r: oh.at[i, r], at_x, along_x, o_box, quarter, base + part_ * quarter) for part_ in range(2)
    ]
    v_ring = Ring(
        lambda i, r: vn.at[i, r, v_cols], at_y, along_y, outbox(vn.at[pl.ds(0, 3), mine, v_cols]), half, base
    )
    vz_ring = Ring(
        lambda i, r: vn.at[:, r, v_part(i)], lambda d: (z + d) % V_PARTS,
        lambda d: dev(dz=1 if d == 1 else NZ - 1), outbox(vn.at[:, mine, pl.ds(0, 3 * v_width)]), half, base,
    )
    v_box = outbox(vn.at[:, mine])
    s_box, l_box = outbox(sg.at[:, pl.ds(0, 3)]), outbox(lb.at[:, pl.ds(0, 3)])
    s_rings, l_rings = [], []
    for t in range(n_chunks):
        q, start = t // CHUNKS, t % CHUNKS * c_rows
        s_rings.append(Ring(lambda i, r, q=q: sg.at[q, i, r], at_y, along_y, s_box, c_rows, start))
        l_rings.append(
            Ring(lambda i, r, q=q, start=start: lb.at[q, i, r, pl.ds(start, c_rows)], at_x, along_x, l_box, NY)
        )

    atoms = pat_ref.shape[0]
    sizes = size_ref[...]
    row = lax.broadcasted_iota(jnp.int32, (blk, atoms), 0) + ao * blk
    row = row - lax.broadcasted_iota(jnp.int32, (blk, atoms), 1) * ATOM_BS
    grow_rows = jnp.where((row >= 0) & (row < sizes), 1.0, 0.0).astype(jnp.bfloat16)
    col = lax.broadcasted_iota(jnp.int32, (ao_total, atoms), 0)
    col = col - lax.broadcasted_iota(jnp.int32, (ao_total, atoms), 1) * ATOM_BS
    grow_cols = jnp.where((col >= 0) & (col < sizes), 1.0, 0.0).astype(jnp.bfloat16)
    pat = pat_ref[...].astype(jnp.float32).astype(jnp.bfloat16)
    pat_rows = jnp.dot(grow_rows, pat, preferred_element_type=jnp.float32).astype(jnp.bfloat16)
    screen = lax.dot_general(pat_rows, grow_cols, NT, preferred_element_type=jnp.float32)
    for b in range(NX * NY):
        scr[b] = screen[:, b * blk:(b + 1) * blk]

    def mask(q):
        for b in range(NX * NY):
            cols = slice(b * blk, (b + 1) * blk)
            sg[q, y, :, cols] = (s_ref[q, :, cols].astype(jnp.float32) * scr[b]).astype(jnp.bfloat16)

    mask(0)
    oh[x] = o_ref[...]
    v_own = pltpu.make_async_copy(v_ref.at[mine, v_cols], vn.at[y, mine, v_cols], lsem.at[1])
    v_own.start()

    o_slots, v_slots, m_slots = [], [], []

    def o_share(part_, d):
        piece = oh.at[at_x(d), pl.ds(base + part_ * quarter, quarter)]
        o_slots.append((part_, d, send(piece, piece, sibling, o_box)))

    def o_join():
        start = (1 - core) * half
        for part_, d, slot in o_slots:
            rows = pl.ds(pl.multiple_of(start + part_ * quarter, quarter), quarter)
            arrived(oh.at[at_x(d), rows], slot)

    def v_share():
        piece = vn.at[:, mine]
        v_slots.append(send(piece, piece, sibling, v_box))

    def v_join():
        arrived(vn.at[:, other], v_slots[-1])

    far_x = at_x(2 * (y // 2))
    far_q = x // 2
    blocks = [at_x(dx) * NY + at_y(dy) for dx, dy in MIRRORED + ((0, 0),)]
    blocks += [far_x * NY + at_y(2), at_x(2) * NY + y]
    m_own, m_other = mb.at[pl.ds(0, ri_rows)], mb.at[pl.ds(ri_rows, ri_rows)]

    def m_start():
        m_slots.append(take())
        box = outbox(m_other)
        for k, b in enumerate(blocks):
            src = m_ref.at[:, :, pl.ds(pl.multiple_of(b * blk, blk), blk)]
            cols = pl.ds(k * blk, blk)
            pltpu.make_async_copy(src, mb.at[pl.ds(0, ri_rows), :, cols], lsem.at[0]).start()
            send(src, mb.at[pl.ds(ri_rows, ri_rows), :, cols], sibling, box, m_slots[0])

    def m_join():
        pltpu.make_async_copy(m_own, m_own, lsem.at[0]).wait()
        arrived(m_other, m_slots[0])

    def left(t):
        q, rows = t // CHUNKS, pl.ds(t % CHUNKS * c_rows, c_rows)
        product = lax.dot_general(
            sg[q, :, rows, :].reshape(NY * c_rows, ao_total), oh[...].reshape(NX * blk, ao_total), NT,
            preferred_element_type=jnp.float32,
        )
        lb[q, x, :, rows, :] = product.astype(jnp.bfloat16).reshape(NY, c_rows, NX * blk)

    def weighted(q):
        product = jnp.dot(
            vn[...].reshape(NY * blk, ao_total), lb[q].reshape(ao_total, NX * blk),
            preferred_element_type=jnp.float32,
        ).astype(jnp.bfloat16)
        for i in range(NX):
            for j in range(NY):
                wb[q, i, j] = product[j * blk:(j + 1) * blk, i * blk:(i + 1) * blk]

    a_slots = {}
    travel = (ab0, ab1)
    wz = (wz0, wz1)

    def exchange(q):
        slot, box = take(), outbox(travel[q])
        a_slots[q] = slot
        along_x_, along_y_ = 0, TRAVEL
        for dx, dy in MIRRORED:
            if dx:
                send(wb.at[q, at_x(NX - dx), at_y(dy)], travel[q].at[along_x_], dev(dx=NX - dx), box, slot)
                along_x_ += 1
            if dy:
                send(wb.at[q, at_x(dx), at_y(NY - dy)], travel[q].at[along_y_], dev(dy=NY - dy), box, slot)
                along_y_ += 1
        send(wb.at[q, at_x(2), at_y(2)], travel[q].at[along_x_], dev(dx=2), box, slot)
        send(wb.at[q, at_x(2 - 2 * (y // 2)), at_y(2)], travel[q].at[along_y_], dev(dy=2), box, slot)
        if q == 1:
            send(wb.at[1 - far_q, at_x(2), y], travel[q].at[2 * TRAVEL], dev(dx=2), box, slot)

    def assemble(q):
        arrived(travel[q], a_slots[q])

        def put(k, block):
            cols = slice(k * blk, (k + 1) * blk)
            wz[q][z, :, cols] = (block * scr[blocks[k]]).astype(jnp.bfloat16)

        def wide(block):
            return block.astype(jnp.float32)

        along_x_, along_y_ = 0, TRAVEL
        for k, (dx, dy) in enumerate(MIRRORED):
            direct = travel[q][along_x_] if dx else wb[q, x, at_y(dy)]
            turned = travel[q][along_y_] if dy else wb[q, at_x(dx), y]
            along_x_, along_y_ = along_x_ + (dx > 0), along_y_ + (dy > 0)
            put(k, wide(direct).T + wide(turned))
        put(len(MIRRORED), wide(wb[q, x, y]).T)
        near = jnp.where(y < 2, 1.0, 0.0)
        direct = wide(wb[q, x, at_y(2)]) * near + wide(travel[q][along_x_]) * (1.0 - near)
        put(len(MIRRORED) + 1, direct.T + wide(travel[q][along_y_]))
        if q == 1:
            put(N_MAIN, wide(travel[q][2 * TRAVEL]).T + wide(wb[far_q, at_x(2), y]))

    gram[...] = jnp.zeros_like(gram)
    pairs = 2 * ri_rows * ROWS

    def contract(*units):
        units = sorted(units)
        second = [d for q, d in units if q == 1]
        main = N_MAIN * blk

        def step(i, totals):
            rows = pl.ds(pl.multiple_of(i * ROWS, ROWS), ROWS)
            b = jnp.concatenate([wz[q][at_z(d), rows, :main] for q, d in units], axis=0)
            a = mb[:, rows, :main].reshape(pairs, main)
            sums = [totals[0] + lax.dot_general(b, a, NT, preferred_element_type=jnp.float32)]
            if second:
                b = jnp.concatenate([wz1[at_z(d), rows, main:] for d in second], axis=0)
                a = mb[:, rows, main:].reshape(pairs, blk)
                sums.append(totals[1] + lax.dot_general(b, a, NT, preferred_element_type=jnp.float32))
            return sums

        heights = [ROWS * len(units)] + [ROWS * len(second)] * bool(second)
        totals = [jnp.zeros((height, pairs), jnp.float32) for height in heights]
        totals = lax.fori_loop(0, blk // ROWS, step, totals, unroll=True)
        places = [units, [(far_q, d) for d in second]]
        for total, where in zip(totals, places):
            i = lax.broadcasted_iota(jnp.int32, total.shape, 0) % ROWS
            j = lax.broadcasted_iota(jnp.int32, total.shape, 1) % ROWS
            total = jnp.where(i == j, total, 0.0)
            for u, (q, d) in enumerate(where):
                kept = jnp.sum(total[u * ROWS:(u + 1) * ROWS], axis=0, keepdims=True)
                row = pl.ds(4 * at_z(d) + 2 * core + q, 1)
                gram[row, :] = gram[row, :] + kept

    z_slots, z_boxes = [{}, {}], [None, None]
    low, high = pl.ds(0, half), pl.ds(half, half)

    halves = (low, high)

    def z_send(q, k, h):
        if (k, h) == (1, 0):
            z_boxes[q] = outbox(wz[q].at[pl.ds(0, NZ - 1)])
        box, last = z_boxes[q], k == NZ // 2
        slot = z_slots[q][k, h] = z_slots[q][k, 0] if last and h else take()
        up, down = wz[q].at[at_z(1 - k), halves[h]], wz[q].at[at_z(k - 1), halves[h]]
        if not last or h == 0:
            send(up, up, dev(dz=1), box, slot)
        if not last or h == 1:
            send(down, down, dev(dz=NZ - 1), box, slot)

    def z_arrived(q, k, h=0):
        arrived(wz[q].at[at_z(k)], z_slots[q][k, h])

    def z_step(q, k, h):
        z_arrived(q, k, h)
        z_send(q, k + 1, h)

    pl.semaphore_wait(barrier, len(partners))
    v_ring.start(v_ref.at[mine, v_cols])
    s_rings[0].start()
    for part_ in range(2):
        rows = pl.ds(pl.multiple_of(base + part_ * quarter, quarter), quarter)
        o_rings[part_].start(o_ref.at[rows])
    s_rings[1].start()
    mask(1)
    o_rings[0].forward()
    for t in range(n_chunks + 3):
        if t < n_chunks:
            s_rings[t].forward()
        if t == 0:
            v_ring.forward()
        if t + 2 < n_chunks:
            s_rings[t + 2].start()
        if t == 0:
            o_share(0, 3)
            o_share(0, 1)
            o_rings[1].forward()
            o_share(1, 3)
            o_share(1, 1)
            o_rings[0].finish()
            o_share(0, 2)
            o_rings[1].finish()
            o_share(1, 2)
        if t == 1:
            o_join()
        if 1 <= t <= n_chunks:
            s_rings[t - 1].finish()
            left(t - 1)
            l_rings[t - 1].start()
        if t == 1:
            v_ring.finish()
            v_own.wait()
            vz_ring.start()
        if t == 3:
            vz_ring.forward()
        if t == 4:
            vz_ring.finish()
            v_share()
        if 2 <= t <= n_chunks + 1:
            l_rings[t - 2].forward()
        if t == CHUNKS + 6:
            z_step(0, 2, 0)
        if 3 <= t:
            l_rings[t - 3].finish()
        if t == 4:
            m_start()
        if t == CHUNKS + 2:
            v_join()
            weighted(0)
            exchange(0)
        if t == CHUNKS + 3:
            assemble(0)
            z_send(0, 1, 0)
            z_send(0, 1, 1)
        if t == CHUNKS + 4:
            z_step(0, 1, 0)
        if t == CHUNKS + 5:
            z_step(0, 1, 1)
    weighted(1)
    exchange(1)
    z_step(0, 2, 1)
    assemble(1)
    z_send(1, 1, 0)
    z_send(1, 1, 1)
    m_join()
    contract((0, 0), (0, 7), (0, 1), (0, 6), (0, 2))
    z_step(0, 3, 0)
    z_step(0, 3, 1)
    z_step(1, 1, 0)
    z_step(1, 1, 1)
    contract((0, 5), (0, 3), (1, 0), (1, 7), (1, 1))
    flush(z_boxes[0] - 1)
    z_step(1, 2, 0)
    z_arrived(0, 4)
    z_step(1, 2, 1)
    contract((0, 4), (1, 6), (1, 2))
    z_step(1, 3, 0)
    z_step(1, 3, 1)
    contract((1, 5), (1, 3))
    flush(z_boxes[0])
    z_arrived(1, 4)
    contract((1, 4),)
    member = lax.broadcasted_iota(jnp.int32, (2 * ri_rows, pairs), 1) // ROWS
    member = member == lax.broadcasted_iota(jnp.int32, (2 * ri_rows, pairs), 0)
    part[...] = lax.dot_general(
        jnp.where(member, 1.0, 0.0), gram[...], NT, precision=lax.Precision.HIGHEST,
        preferred_element_type=jnp.float32,
    )

    own, theirs = part.at[pl.ds(0, ri_rows)], part.at[pl.ds(ri_rows, ri_rows)]
    red_x[core, x] = part[:ri_rows]
    place = red_x.at[core, x]
    near, far = take(), take()
    near_box, far_box = outbox(red_x.at[0, pl.ds(0, 3)]), outbox(red_x.at[0])
    for d in (1, 2, 3):
        send(own, place, dev(dx=d), near_box, near)
    for d in range(NX):
        send(theirs, place, other_core(d), far_box, far)
    arrived(red_x.at[core, pl.ds(0, 3)], near)
    arrived(red_x.at[1 - core], far)
    red_y[y] = functools.reduce(jnp.add, [red_x[i, j] for i in range(2) for j in range(NX)])
    slot, box = take(), outbox(red_y.at[pl.ds(0, 3)])
    for d in (1, 2, 3):
        send(red_y.at[y], red_y.at[y], dev(dy=d), box, slot)
    arrived(red_y.at[pl.ds(0, 3)], slot)
    total = red_y[0] + red_y[1] + red_y[2] + red_y[3]
    out_ref[...] = total[:, :out_ref.shape[1]] / ao_total
    flush()
    assert (landed[0], len(boxes)) == (ARRIVALS, BOXES), (landed, len(boxes))


def shards(three_center, slab_tensor, occ_green, virt_green, pattern, atom_sizes):
    ri_rows, blk, ao_total = three_center.shape
    bf16, f32 = jnp.bfloat16, jnp.float32
    vmem = pl.BlockSpec(memory_space=pltpu.VMEM)
    columns = 4 * NZ
    return pl.pallas_call(
        kernel,
        out_shape=jax.ShapeDtypeStruct((ri_rows, columns), f32),
        in_specs=[pl.BlockSpec(memory_space=pl.ANY)] + [vmem] * 5,
        out_specs=vmem,
        scratch_shapes=[
            pltpu.VMEM((NX, blk, ao_total), bf16),
            pltpu.VMEM((NY, blk, ao_total), bf16),
            pltpu.VMEM((2, NY, blk, ao_total), bf16),
            pltpu.VMEM((2, NX, NY, blk, NX * blk), bf16),
            pltpu.VMEM((2, NX, NY, blk, blk), bf16),
            pltpu.VMEM((2 * TRAVEL, blk, blk), bf16),
            pltpu.VMEM((2 * TRAVEL + 1, blk, blk), bf16),
            pltpu.VMEM((NZ, blk, N_MAIN * blk), bf16),
            pltpu.VMEM((NZ, blk, N_OWNED * blk), bf16),
            pltpu.VMEM((2 * ri_rows, blk, N_OWNED * blk), bf16),
            pltpu.VMEM((NX * NY, blk, blk), f32),
            pltpu.VMEM((128, 2 * ri_rows * ROWS), f32),
            pltpu.VMEM((2 * ri_rows, 128), f32),
            pltpu.VMEM((2, NX, ri_rows, 128), f32),
            pltpu.VMEM((NY, ri_rows, 128), f32),
            pltpu.SemaphoreType.DMA((BOXES,)),
            pltpu.SemaphoreType.DMA((ARRIVALS,)),
            pltpu.SemaphoreType.DMA((2,)),
        ],
        compiler_params=pltpu.CompilerParams(
            collective_id=0, has_side_effects=True, vmem_limit_bytes=60 * 1024 * 1024
        ),
        name="polar_slab",
    )(three_center, slab_tensor, occ_green, virt_green, pattern, atom_sizes.reshape(1, -1))


def solution(mesh):
    placed = (P("ri", "ao", None), P("ri", "ao", None), P("ao", None), P("ao", None), P(), P())
    return jax.shard_map(
        shards, mesh=mesh, in_specs=placed, out_specs=P("ri", None), check_vma=False
    )
```

```python
import functools

import jax
import jax.numpy as jnp
from jax import lax
from jax.experimental import pallas as pl
from jax.experimental.pallas import tpu as pltpu
from jax.sharding import PartitionSpec as P

MESH = pl.DeviceIdType.MESH
ATOM_BS = 16
NX, NY, NZ = 4, 4, 8
ROWS = 16
CHUNKS = 4
ARRIVALS, BOXES = 87, 14
V_PARTS = 4

MIRRORED = ((1, 0), (1, 1), (1, 3), (1, 2), (0, 1), (2, 1))
N_MAIN = len(MIRRORED) + 2
N_OWNED = N_MAIN + 1
TRAVEL = 6
NT = (((1,), (1,)), ((), ()))


def kernel(
    m_ref, s_ref, o_ref, v_ref, pat_ref, size_ref, out_ref,
    oh, vn, sg, lb, wb, ab0, ab1, wz0, wz1, mb, scr, gram, part, red_x, red_y,
    ssem, rsem, lsem,
):
    blk, ao_total = o_ref.shape
    ri_rows = m_ref.shape[0]
    ri, ao = lax.axis_index("ri"), lax.axis_index("ao")
    z, core = ri // 2, ri % 2
    x, y = ao // NY, ao % NY

    def at_x(d):
        return (x + d) % NX

    def at_y(d):
        return (y + d) % NY

    def at_z(d):
        return (z + d) % NZ

    def dev(dx=0, dy=0, dz=0):
        return (at_z(dz) * 2 + core, at_x(dx) * NY + at_y(dy))

    def other_core(dx):
        return (z * 2 + 1 - core, at_x(dx) * NY + y)

    sibling = (z * 2 + 1 - core, ao)
    half = blk // 2
    mine = pl.ds(pl.multiple_of(core * half, half), half)

    landed, boxes, emptied = [0], [], [0]

    def remote(src, dst, device, slot, box):
        return pltpu.make_async_remote_copy(
            src_ref=src, dst_ref=dst, send_sem=ssem.at[box], recv_sem=rsem.at[slot],
            device_id=device, device_id_type=MESH,
        )

    def outbox(whole):
        boxes.append(whole)
        return len(boxes) - 1

    def take():
        landed[0] += 1
        return landed[0] - 1

    def send(src, dst, device, box, slot=None):
        slot = take() if slot is None else slot
        remote(src, dst, device, slot, box).start()
        return slot

    def flush(last=None):
        for box in range(emptied[0], len(boxes) if last is None else last + 1):
            remote(boxes[box], boxes[box], sibling, 0, box).wait_send()
            emptied[0] = box + 1

    def arrived(ref, slot):
        remote(ref, ref, sibling, slot, 0).wait_recv()

    barrier = pltpu.get_barrier_semaphore()
    partners = [dev(dx=1), dev(dx=2), dev(dx=3), dev(dy=1), dev(dy=2), dev(dy=3), sibling]
    partners += [dev(dz=1), dev(dz=7)]
    partners += [other_core(1), other_core(2), other_core(3)]
    for partner in partners:
        pl.semaphore_signal(barrier, inc=1, device_id=partner, device_id_type=MESH)

    class Ring:
        def __init__(self, view, at, device, box, rows, start=0):
            self.view, self.at, self.device, self.box = view, at, device, box
            self.low = pl.ds(start, rows // 2)
            self.high = pl.ds(start + rows // 2, rows // 2)
            self.all = pl.ds(start, rows)

        def start(self, src=None):
            block = self.view(self.at(0), self.all)
            src = block if src is None else src
            self.a = send(src, block, self.device(1), self.box)
            self.b = send(src, block, self.device(3), self.box)

        def forward(self):
            arrived(self.view(self.at(3), self.all), self.a)
            piece = self.view(self.at(3), self.low)
            self.c = send(piece, piece, self.device(1), self.box)
            arrived(self.view(self.at(1), self.all), self.b)
            piece = self.view(self.at(1), self.high)
            send(piece, piece, self.device(3), self.box, self.c)

        def finish(self):
            arrived(self.view(self.at(2), self.all), self.c)

    def along_x(d):
        return dev(dx=d)

    def along_y(d):
        return dev(dy=d)

    base = pl.multiple_of(core * half, half)
    other = pl.ds(pl.multiple_of((1 - core) * half, half), half)
    v_width = ao_total // V_PARTS

    def v_part(i):
        return pl.ds(pl.multiple_of(i * v_width, v_width), v_width)

    v_cols = v_part(z % V_PARTS)
    c_rows = blk // CHUNKS
    n_chunks = 2 * CHUNKS

    quarter = half // 2
    o_box = outbox(oh.at[pl.ds(0, 3)])
    o_rings = [
        Ring(lambda i, r: oh.at[i, r], at_x, along_x, o_box, quarter, base + part_ * quarter) for part_ in range(2)
    ]
    v_ring = Ring(
        lambda i, r: vn.at[i, r, v_cols], at_y, along_y, outbox(vn.at[pl.ds(0, 3), mine, v_cols]), half, base
    )
    vz_ring = Ring(
        lambda i, r: vn.at[:, r, v_part(i)], lambda d: (z + d) % V_PARTS,
        lambda d: dev(dz=1 if d == 1 else NZ - 1), outbox(vn.at[:, mine, pl.ds(0, 3 * v_width)]), half, base,
    )
    v_box = outbox(vn.at[:, mine])
    s_box, l_box = outbox(sg.at[:, pl.ds(0, 3)]), outbox(lb.at[:, pl.ds(0, 3)])
    s_rings, l_rings = [], []
    for t in range(n_chunks):
        q, start = t // CHUNKS, t % CHUNKS * c_rows
        s_rings.append(Ring(lambda i, r, q=q: sg.at[q, i, r], at_y, along_y, s_box, c_rows, start))
        l_rings.append(
            Ring(lambda i, r, q=q, start=start: lb.at[q, i, r, pl.ds(start, c_rows)], at_x, along_x, l_box, NY)
        )

    atoms = pat_ref.shape[0]
    sizes = size_ref[...]
    row = lax.broadcasted_iota(jnp.int32, (blk, atoms), 0) + ao * blk
    row = row - lax.broadcasted_iota(jnp.int32, (blk, atoms), 1) * ATOM_BS
    grow_rows = jnp.where((row >= 0) & (row < sizes), 1.0, 0.0).astype(jnp.bfloat16)
    col = lax.broadcasted_iota(jnp.int32, (ao_total, atoms), 0)
    col = col - lax.broadcasted_iota(jnp.int32, (ao_total, atoms), 1) * ATOM_BS
    grow_cols = jnp.where((col >= 0) & (col < sizes), 1.0, 0.0).astype(jnp.bfloat16)
    pat = pat_ref[...].astype(jnp.float32).astype(jnp.bfloat16)
    pat_rows = jnp.dot(grow_rows, pat, preferred_element_type=jnp.float32).astype(jnp.bfloat16)
    screen = lax.dot_general(pat_rows, grow_cols, NT, preferred_element_type=jnp.float32)
    for b in range(NX * NY):
        scr[b] = screen[:, b * blk:(b + 1) * blk]

    def mask(q):
        for b in range(NX * NY):
            cols = slice(b * blk, (b + 1) * blk)
            sg[q, y, :, cols] = (s_ref[q, :, cols].astype(jnp.float32) * scr[b]).astype(jnp.bfloat16)

    mask(0)
    oh[x] = o_ref[...]
    v_own = pltpu.make_async_copy(v_ref.at[mine, v_cols], vn.at[y, mine, v_cols], lsem.at[1])
    v_own.start()

    o_slots, v_slots, m_slots = [], [], []

    def o_share(part_, d):
        piece = oh.at[at_x(d), pl.ds(base + part_ * quarter, quarter)]
        o_slots.append((part_, d, send(piece, piece, sibling, o_box)))

    def o_join():
        start = (1 - core) * half
        for part_, d, slot in o_slots:
            rows = pl.ds(pl.multiple_of(start + part_ * quarter, quarter), quarter)
            arrived(oh.at[at_x(d), rows], slot)

    def v_share():
        piece = vn.at[:, mine]
        v_slots.append(send(piece, piece, sibling, v_box))

    def v_join():
        arrived(vn.at[:, other], v_slots[-1])

    far_x = at_x(2 * (y // 2))
    far_q = x // 2
    blocks = [at_x(dx) * NY + at_y(dy) for dx, dy in MIRRORED + ((0, 0),)]
    blocks += [far_x * NY + at_y(2), at_x(2) * NY + y]
    m_own, m_other = mb.at[pl.ds(0, ri_rows)], mb.at[pl.ds(ri_rows, ri_rows)]

    def m_start():
        m_slots.append(take())
        box = outbox(m_other)
        for k, b in enumerate(blocks):
            src = m_ref.at[:, :, pl.ds(pl.multiple_of(b * blk, blk), blk)]
            cols = pl.ds(k * blk, blk)
            pltpu.make_async_copy(src, mb.at[pl.ds(0, ri_rows), :, cols], lsem.at[0]).start()
            send(src, mb.at[pl.ds(ri_rows, ri_rows), :, cols], sibling, box, m_slots[0])

    def m_join():
        pltpu.make_async_copy(m_own, m_own, lsem.at[0]).wait()
        arrived(m_other, m_slots[0])

    def left(t):
        q, rows = t // CHUNKS, pl.ds(t % CHUNKS * c_rows, c_rows)
        product = lax.dot_general(
            sg[q, :, rows, :].reshape(NY * c_rows, ao_total), oh[...].reshape(NX * blk, ao_total), NT,
            preferred_element_type=jnp.float32,
        )
        lb[q, x, :, rows, :] = product.astype(jnp.bfloat16).reshape(NY, c_rows, NX * blk)

    def weighted(q):
        product = jnp.dot(
            vn[...].reshape(NY * blk, ao_total), lb[q].reshape(ao_total, NX * blk),
            preferred_element_type=jnp.float32,
        ).astype(jnp.bfloat16)
        for i in range(NX):
            for j in range(NY):
                wb[q, i, j] = product[j * blk:(j + 1) * blk, i * blk:(i + 1) * blk]

    a_slots = {}
    travel = (ab0, ab1)
    wz = (wz0, wz1)

    def exchange(q):
        slot, box = take(), outbox(travel[q])
        a_slots[q] = slot
        along_x_, along_y_ = 0, TRAVEL
        for dx, dy in MIRRORED:
            if dx:
                send(wb.at[q, at_x(NX - dx), at_y(dy)], travel[q].at[along_x_], dev(dx=NX - dx), box, slot)
                along_x_ += 1
            if dy:
                send(wb.at[q, at_x(dx), at_y(NY - dy)], travel[q].at[along_y_], dev(dy=NY - dy), box, slot)
                along_y_ += 1
        send(wb.at[q, at_x(2), at_y(2)], travel[q].at[along_x_], dev(dx=2), box, slot)
        send(wb.at[q, at_x(2 - 2 * (y // 2)), at_y(2)], travel[q].at[along_y_], dev(dy=2), box, slot)
        if q == 1:
            send(wb.at[1 - far_q, at_x(2), y], travel[q].at[2 * TRAVEL], dev(dx=2), box, slot)

    def assemble(q):
        arrived(travel[q], a_slots[q])

        def put(k, block):
            cols = slice(k * blk, (k + 1) * blk)
            wz[q][z, :, cols] = (block * scr[blocks[k]]).astype(jnp.bfloat16)

        def wide(block):
            return block.astype(jnp.float32)

        along_x_, along_y_ = 0, TRAVEL
        for k, (dx, dy) in enumerate(MIRRORED):
            direct = travel[q][along_x_] if dx else wb[q, x, at_y(dy)]
            turned = travel[q][along_y_] if dy else wb[q, at_x(dx), y]
            along_x_, along_y_ = along_x_ + (dx > 0), along_y_ + (dy > 0)
            put(k, wide(direct).T + wide(turned))
        put(len(MIRRORED), wide(wb[q, x, y]).T)
        near = jnp.where(y < 2, 1.0, 0.0)
        direct = wide(wb[q, x, at_y(2)]) * near + wide(travel[q][along_x_]) * (1.0 - near)
        put(len(MIRRORED) + 1, direct.T + wide(travel[q][along_y_]))
        if q == 1:
            put(N_MAIN, wide(travel[q][2 * TRAVEL]).T + wide(wb[far_q, at_x(2), y]))

    gram[...] = jnp.zeros_like(gram)
    pairs = 2 * ri_rows * ROWS

    def contract(*units):
        units = sorted(units)
        second = [d for q, d in units if q == 1]
        main = N_MAIN * blk

        def step(i, totals):
            rows = pl.ds(pl.multiple_of(i * ROWS, ROWS), ROWS)
            b = jnp.concatenate([wz[q][at_z(d), rows, :main] for q, d in units], axis=0)
            a = mb[:, rows, :main].reshape(pairs, main)
            sums = [totals[0] + lax.dot_general(b, a, NT, preferred_element_type=jnp.float32)]
            if second:
                b = jnp.concatenate([wz1[at_z(d), rows, main:] for d in second], axis=0)
                a = mb[:, rows, main:].reshape(pairs, blk)
                sums.append(totals[1] + lax.dot_general(b, a, NT, preferred_element_type=jnp.float32))
            return sums

        heights = [ROWS * len(units)] + [ROWS * len(second)] * bool(second)
        totals = [jnp.zeros((height, pairs), jnp.float32) for height in heights]
        totals = lax.fori_loop(0, blk // ROWS, step, totals, unroll=True)
        places = [units, [(far_q, d) for d in second]]
        for total, where in zip(totals, places):
            i = lax.broadcasted_iota(jnp.int32, total.shape, 0) % ROWS
            j = lax.broadcasted_iota(jnp.int32, total.shape, 1) % ROWS
            total = jnp.where(i == j, total, 0.0)
            for u, (q, d) in enumerate(where):
                kept = jnp.sum(total[u * ROWS:(u + 1) * ROWS], axis=0, keepdims=True)
                row = pl.ds(4 * at_z(d) + 2 * core + q, 1)
                gram[row, :] = gram[row, :] + kept

    z_slots, z_boxes = [{}, {}], [None, None]
    low, high = pl.ds(0, half), pl.ds(half, half)

    halves = (low, high)

    def z_send(q, k, h):
        if (k, h) == (1, 0):
            z_boxes[q] = outbox(wz[q].at[pl.ds(0, NZ - 1)])
        box, last = z_boxes[q], k == NZ // 2
        slot = z_slots[q][k, h] = z_slots[q][k, 0] if last and h else take()
        up, down = wz[q].at[at_z(1 - k), halves[h]], wz[q].at[at_z(k - 1), halves[h]]
        if not last or h == 0:
            send(up, up, dev(dz=1), box, slot)
        if not last or h == 1:
            send(down, down, dev(dz=NZ - 1), box, slot)

    def z_arrived(q, k, h=0):
        arrived(wz[q].at[at_z(k)], z_slots[q][k, h])

    def z_step(q, k, h):
        z_arrived(q, k, h)
        z_send(q, k + 1, h)

    pl.semaphore_wait(barrier, len(partners))
    v_ring.start(v_ref.at[mine, v_cols])
    s_rings[0].start()
    for part_ in range(2):
        rows = pl.ds(pl.multiple_of(base + part_ * quarter, quarter), quarter)
        o_rings[part_].start(o_ref.at[rows])
    s_rings[1].start()
    mask(1)
    o_rings[0].forward()
    for t in range(n_chunks + 3):
        if t < n_chunks:
            s_rings[t].forward()
        if t == 0:
            v_ring.forward()
        if t + 2 < n_chunks:
            s_rings[t + 2].start()
        if t == 0:
            o_share(0, 3)
            o_share(0, 1)
            o_rings[1].forward()
            o_share(1, 3)
            o_share(1, 1)
            o_rings[0].finish()
            o_share(0, 2)
            o_rings[1].finish()
            o_share(1, 2)
        if t == 1:
            o_join()
        if 1 <= t <= n_chunks:
            s_rings[t - 1].finish()
            left(t - 1)
            l_rings[t - 1].start()
        if t == 1:
            v_ring.finish()
            v_own.wait()
            vz_ring.start()
        if t == 3:
            vz_ring.forward()
        if t == 4:
            vz_ring.finish()
            v_share()
        if 2 <= t <= n_chunks + 1:
            l_rings[t - 2].forward()
        if t == CHUNKS + 6:
            z_step(0, 2, 0)
        if 3 <= t:
            l_rings[t - 3].finish()
        if t == 4:
            m_start()
        if t == CHUNKS + 2:
            v_join()
            weighted(0)
            exchange(0)
        if t == CHUNKS + 3:
            assemble(0)
            z_send(0, 1, 0)
            z_send(0, 1, 1)
        if t == CHUNKS + 4:
            z_step(0, 1, 0)
        if t == CHUNKS + 5:
            z_step(0, 1, 1)
    weighted(1)
    exchange(1)
    z_step(0, 2, 1)
    z_step(0, 3, 0)
    assemble(1)
    z_send(1, 1, 0)
    z_send(1, 1, 1)
    m_join()
    contract((0, 0), (0, 7), (0, 1), (0, 6), (0, 2))
    z_step(0, 3, 1)
    z_step(1, 1, 0)
    z_step(1, 1, 1)
    contract((0, 5), (0, 3), (1, 0), (1, 7), (1, 1))
    flush(z_boxes[0] - 1)
    z_step(1, 2, 0)
    z_arrived(0, 4)
    z_step(1, 2, 1)
    contract((0, 4), (1, 6), (1, 2))
    z_step(1, 3, 0)
    z_step(1, 3, 1)
    contract((1, 5), (1, 3))
    flush(z_boxes[0])
    z_arrived(1, 4)
    contract((1, 4),)
    member = lax.broadcasted_iota(jnp.int32, (2 * ri_rows, pairs), 1) // ROWS
    member = member == lax.broadcasted_iota(jnp.int32, (2 * ri_rows, pairs), 0)
    part[...] = lax.dot_general(
        jnp.where(member, 1.0, 0.0), gram[...], NT, precision=lax.Precision.HIGHEST,
        preferred_element_type=jnp.float32,
    )

    own, theirs = part.at[pl.ds(0, ri_rows)], part.at[pl.ds(ri_rows, ri_rows)]
    red_x[core, x] = part[:ri_rows]
    place = red_x.at[core, x]
    near, far = take(), take()
    near_box, far_box = outbox(red_x.at[0, pl.ds(0, 3)]), outbox(red_x.at[0])
    for d in (1, 2, 3):
        send(own, place, dev(dx=d), near_box, near)
    for d in range(NX):
        send(theirs, place, other_core(d), far_box, far)
    arrived(red_x.at[core, pl.ds(0, 3)], near)
    arrived(red_x.at[1 - core], far)
    red_y[y] = functools.reduce(jnp.add, [red_x[i, j] for i in range(2) for j in range(NX)])
    slot, box = take(), outbox(red_y.at[pl.ds(0, 3)])
    for d in (1, 2, 3):
        send(red_y.at[y], red_y.at[y], dev(dy=d), box, slot)
    arrived(red_y.at[pl.ds(0, 3)], slot)
    total = red_y[0] + red_y[1] + red_y[2] + red_y[3]
    out_ref[...] = total[:, :out_ref.shape[1]] / ao_total
    flush()
    assert (landed[0], len(boxes)) == (ARRIVALS, BOXES), (landed, len(boxes))


def shards(three_center, slab_tensor, occ_green, virt_green, pattern, atom_sizes):
    ri_rows, blk, ao_total = three_center.shape
    bf16, f32 = jnp.bfloat16, jnp.float32
    vmem = pl.BlockSpec(memory_space=pltpu.VMEM)
    columns = 4 * NZ
    return pl.pallas_call(
        kernel,
        out_shape=jax.ShapeDtypeStruct((ri_rows, columns), f32),
        in_specs=[pl.BlockSpec(memory_space=pl.ANY)] + [vmem] * 5,
        out_specs=vmem,
        scratch_shapes=[
            pltpu.VMEM((NX, blk, ao_total), bf16),
            pltpu.VMEM((NY, blk, ao_total), bf16),
            pltpu.VMEM((2, NY, blk, ao_total), bf16),
            pltpu.VMEM((2, NX, NY, blk, NX * blk), bf16),
            pltpu.VMEM((2, NX, NY, blk, blk), bf16),
            pltpu.VMEM((2 * TRAVEL, blk, blk), bf16),
            pltpu.VMEM((2 * TRAVEL + 1, blk, blk), bf16),
            pltpu.VMEM((NZ, blk, N_MAIN * blk), bf16),
            pltpu.VMEM((NZ, blk, N_OWNED * blk), bf16),
            pltpu.VMEM((2 * ri_rows, blk, N_OWNED * blk), bf16),
            pltpu.VMEM((NX * NY, blk, blk), f32),
            pltpu.VMEM((128, 2 * ri_rows * ROWS), f32),
            pltpu.VMEM((2 * ri_rows, 128), f32),
            pltpu.VMEM((2, NX, ri_rows, 128), f32),
            pltpu.VMEM((NY, ri_rows, 128), f32),
            pltpu.SemaphoreType.DMA((BOXES,)),
            pltpu.SemaphoreType.DMA((ARRIVALS,)),
            pltpu.SemaphoreType.DMA((2,)),
        ],
        compiler_params=pltpu.CompilerParams(
            collective_id=0, has_side_effects=True, vmem_limit_bytes=60 * 1024 * 1024
        ),
        name="polar_slab",
    )(three_center, slab_tensor, occ_green, virt_green, pattern, atom_sizes.reshape(1, -1))


def solution(mesh):
    placed = (P("ri", "ao", None), P("ri", "ao", None), P("ao", None), P("ao", None), P(), P())
    return jax.shard_map(
        shards, mesh=mesh, in_specs=placed, out_specs=P("ri", None), check_vma=False
    )
```
